256 devices in a mesh: pts: 128 (over y, x, z_hi, core), rhs: 2 (over z_lo).
Axes of the slice: x: 4, y: 4, z: 8 (z_hi: 4, z_lo: 2; z = z_hi * 2 + z_lo), core: 2. Of those that a mesh axis runs over, the one named last changes fastest.
Arguments:
- right_sides: bfloat16 [64, 524288], P('rhs', 'pts'), may hold values from -6 to 6
- morton: int32 [524288], P('pts'), may hold values from 0 to 524287, as said below
- near_leaf: int32 [256], P('pts'), may hold values from 0 to 255, as said below
- points: bfloat16 [64, 524288], P(None, 'pts'), may hold values from -5 to 5
- far_left: bfloat16 [8, 64, 524288], P(None, None, 'pts'), may hold values from -0.25 to 0.25
- far_right: bfloat16 [8, 64, 524288], P(None, None, 'pts'), may hold values from -4 to 4, as said below
Outputs:
- first_product: float32 [64, 524288], P('rhs', 'pts')
- second_product: float32 [64, 524288], P('rhs', 'pts')
The draws below stay inside these ranges and needn't reach their ends.
Inputs may be any that keep to these rules, and one draw needn't show every extreme that they name: `morton`: each block of 4096 consecutive entries holds the indices of that same block in some order. `near_leaf`: for an even leaf i the entry is i - 1 or i - 2, for an odd leaf i + 1 or i + 2, clipped to the range of leaves. `far_right`: entries of level k are at most 4 / sqrt(2048 * 2^k) in magnitude.
All inputs are finite; a program needn't handle non-finite values.
Results may differ from the reference program's by a relative error of at most 0.0028.
Values may be sent and summed in bfloat16 or wider, within the bound.
A program may use at most 128 MiB of HBM per device.

```python
import jax
import jax.numpy as jnp
from jax import lax

DIM = 64
R = 64
LEAF = 2048
C = 64
POINTS_DEV = 4096
NPTS = 524288
LEAVES = 256
LEVELS = 8


def draw_morton(key, part):
    key = jax.random.fold_in(key, 11)
    block_count = NPTS // POINTS_DEV
    block_keys = jax.random.split(key, block_count)
    inside = jax.vmap(lambda block_key: jax.random.permutation(block_key, POINTS_DEV))(block_keys)
    offsets = jnp.arange(block_count, dtype=jnp.int32)[:, None] * POINTS_DEV
    return (inside.astype(jnp.int32) + offsets).reshape(NPTS).astype(jnp.int32)


def draw_near_leaf(key, part):
    key = jax.random.fold_in(key, 23)
    coin_flips = jax.random.randint(key, (LEAVES,), 0, 2, dtype=jnp.int32)
    leaf_index = jnp.arange(LEAVES, dtype=jnp.int32)
    partner = jnp.where(leaf_index % 2 == 0, leaf_index - 1 - coin_flips, leaf_index + 1 + coin_flips)
    return jnp.clip(partner, 0, LEAVES - 1).astype(jnp.int32)


def draw_far_right(key, part):
    key = jax.random.fold_in(key, 37)
    level_scale = jnp.power(LEAF * jnp.power(2.0, jnp.arange(LEVELS, dtype=jnp.float32)), -0.5)
    base_values = jax.random.truncated_normal(key, -4.0, 4.0, (LEVELS, R, NPTS), jnp.float32)
    return (base_values * level_scale[:, None, None]).astype(jnp.bfloat16)


def block_levels(rng, dims, shards, smallest, top_value):
    level = 1.0
    for dim, parts in shards:
        draws = jax.random.uniform(jax.random.fold_in(jax.random.fold_in(rng, 6), dim), (parts,), jnp.float32, smallest / len(shards), top_value / len(shards))
        level = level * jnp.repeat(jnp.exp(draws), dims[dim] // parts).reshape((-1,) + (1,) * (len(dims) - 1 - dim))
    return level


def scatter_about(rng, extent, spread, reach, cuts=(), kind=jnp.bfloat16):
    values = spread * jax.random.normal(rng, extent, jnp.float32)
    if cuts:
        values = values * block_levels(rng, extent, cuts, -0.22, 0.18)
    return jnp.clip(values, -reach, reach).astype(kind)


def setup_inputs(seed: int = 0) -> dict:
    splits = jax.random.split(jax.random.key(seed), 7)
    right_sides = scatter_about(splits[0], (C, NPTS), 1.0, 6.0, ((0, 2), (1, 128)))
    morton = draw_morton(jax.random.fold_in(splits[6], 71), 0)
    near_leaf = draw_near_leaf(jax.random.fold_in(splits[6], 71), 0)
    points = scatter_about(splits[3], (DIM, NPTS), 1.0, 5.0, ((1, 128),))
    far_left = scatter_about(splits[4], (LEVELS, R, NPTS), (R * LEVELS) ** -0.5, 0.25, ((2, 128),))
    far_right = draw_far_right(jax.random.fold_in(splits[6], 71), 0)
    return {"right_sides": right_sides, "morton": morton, "near_leaf": near_leaf, "points": points, "far_left": far_left, "far_right": far_right}


def kernel_tile(source, target):
    inner_products = jnp.dot(source.T, target, preferred_element_type=jnp.float32)
    source_sq = jnp.sum(jnp.square(source.astype(jnp.float32)), axis=0)
    target_sq = jnp.sum(jnp.square(target.astype(jnp.float32)), axis=0)
    distance = source_sq[:, None] + target_sq[None, :] - 2.0 * inner_products
    return jnp.exp(-(distance * (2.0 / DIM))).astype(jnp.bfloat16)


def apply_operator(values, near_leaf, points, far_left, far_right):
    def leaf_term(leaf_index):
        own_start = (leaf_index * LEAF).astype(jnp.int32)
        other_start = (near_leaf[leaf_index] * LEAF).astype(jnp.int32)
        own_points = lax.dynamic_slice_in_dim(points, own_start, LEAF, 1)
        other_points = lax.dynamic_slice_in_dim(points, other_start, LEAF, 1)
        own_values = lax.dynamic_slice_in_dim(values, own_start, LEAF, 1)
        other_values = lax.dynamic_slice_in_dim(values, other_start, LEAF, 1)
        near_sum = jnp.dot(own_values, kernel_tile(own_points, own_points), preferred_element_type=jnp.float32)
        return near_sum + jnp.dot(other_values, kernel_tile(other_points, own_points), preferred_element_type=jnp.float32)

    near_terms = lax.map(leaf_term, jnp.arange(LEAVES, dtype=jnp.int32))
    near_sum = jnp.transpose(near_terms, (1, 0, 2)).reshape(C, NPTS)
    wide_values = values.astype(jnp.float32)
    far_sum = jnp.zeros((C, NPTS), jnp.float32)
    for level_index in range(LEVELS):
        node_size = LEAF * 2 ** level_index
        node_count = NPTS // node_size
        right_factor = far_right[level_index].astype(jnp.float32).reshape(R, node_count, node_size)
        grouped = wide_values.reshape(C, node_count, node_size)
        coefficients = jnp.einsum("rnp,cnp->nrc", right_factor, grouped, precision=lax.Precision.HIGHEST)
        swapped = coefficients.reshape(node_count // 2, 2, R, C)[:, ::-1].reshape(node_count, R, C)
        sibling = lax.optimization_barrier(swapped.astype(jnp.bfloat16)).astype(jnp.float32)
        left_factor = far_left[level_index].astype(jnp.float32).reshape(R, node_count, node_size)
        far_sum = far_sum + jnp.einsum("nrc,rnp->cnp", sibling, left_factor, precision=lax.Precision.HIGHEST).reshape(C, NPTS)
    return near_sum + far_sum


def reference(right_sides, morton, near_leaf, points, far_left, far_right):
    ordered = jnp.take(right_sides, morton, axis=1)
    first_product = apply_operator(ordered, near_leaf, points, far_left, far_right)
    carried = first_product.astype(jnp.bfloat16)
    second_product = apply_operator(carried, near_leaf, points, far_left, far_right)
    return first_product, second_product
```

```python
import jax
import jax.numpy as jnp
from jax import lax
from jax.experimental import pallas as pl
from jax.experimental.pallas import tpu as pltpu
from jax.sharding import PartitionSpec as P

DIM = 64
LEAF = 2048
RANK = 64
LEVELS = 8
ROWS = 32
HALF = 16
WIDTH = LEVELS * RANK
BLOCK = 2 * LEAF
DEPTH = 128
MESH = pl.DeviceIdType.MESH
F32 = jnp.float32
BF16 = jnp.bfloat16


def dot(a, b):
    return jnp.dot(a, b, preferred_element_type=F32)


def dot_nt(a, b):
    return lax.dot_general(a, b, (((1,), (1,)), ((), ())), preferred_element_type=F32)


def norm_rows(x, first):
    wide = x.astype(F32)
    a = jnp.sum(wide * wide, axis=0, keepdims=True) * (-1.0 / 32.0)
    h1 = a.astype(BF16).astype(F32)
    r1 = a - h1
    h2 = r1.astype(BF16).astype(F32)
    h3 = r1 - h2
    row = lax.broadcasted_iota(jnp.int32, (8, x.shape[1]), 0) - first
    one = jnp.where((row >= 3 - 2 * first) & (row < 6 - 2 * first), 1.0, 0.0)
    return jnp.where(row == 0, h1, jnp.where(row == 1, h2, jnp.where(row == 2, h3, one)))


def kernel(
    near, morton, rs_hbm, pts_hbm, fl_hbm, fr_hbm,
    out1, out2,
    tiles, fl, fr, pts, halo_pts, stage_pts, rs, vals, halo_vals, stage_vals,
    src, tgt, acc, far_sum, sel_out, sel_in,
    coef, p0_in, p1_out, p1_in, p2_out, p2_in, p3_out, p3_in, sib_half, sib,
    local_sem, out_sem, send_sem, recv_sem,
):
    pos = lax.axis_index("pts")
    count = lax.axis_size("pts")
    left = lax.rem(pos + count - 1, count)
    right = lax.rem(pos + 1, count)
    core = lax.rem(pos, 2)
    mate = pos + 1 - 2 * core

    def partner(shift, d):
        digit = lax.rem(pos // shift, 4)
        if d == 1:
            other = digit + 1 - 2 * lax.rem(digit, 2)
        elif d == 2:
            other = lax.rem(digit + 2, 4)
        else:
            other = 3 - digit
        return pos + (other - digit) * shift

    peers = {ax: [partner(shift, d) for d in (1, 2, 3)] for ax, shift in (("z", 2), ("x", 8), ("y", 32))}

    load_rs = pltpu.make_async_copy(rs_hbm, rs, local_sem.at[0])
    load_pts = [
        pltpu.make_async_copy(pts_hbm.at[:, pl.ds(l * LEAF, LEAF)], pts.at[l], local_sem.at[1 + l]) for l in range(2)
    ]
    load_fr = pltpu.make_async_copy(fr_hbm, fr, local_sem.at[3])
    load_fl = pltpu.make_async_copy(fl_hbm, fl, local_sem.at[4])
    load_rs.start()
    load_pts[0].start()
    load_pts[1].start()
    load_fr.start()
    load_fl.start()

    barrier = pltpu.get_barrier_semaphore()
    everyone = [left, right, mate] + peers["z"] + peers["x"] + peers["y"]
    for peer in everyone:
        pl.semaphore_signal(barrier, inc=1, device_id={"pts": peer}, device_id_type=MESH)

    slot = [0]
    sent = []

    def remote(source, target, peer):
        i = slot[0]
        slot[0] += 1
        copy = pltpu.make_async_remote_copy(
            src_ref=source, dst_ref=target, send_sem=send_sem.at[i], recv_sem=recv_sem.at[i],
            device_id={"pts": peer}, device_id_type=MESH,
        )
        sent.append(copy)
        return copy

    sel_out[0] = jnp.full((8, 128), (near[0] - 2 * pos + 2).astype(F32))
    sel_out[1] = jnp.full((8, 128), (near[1] - 2 * pos - 2).astype(F32))

    load_rs.wait()
    folded = jnp.concatenate([rs[:, h * 256 : (h + 1) * 256] for h in range(16)], axis=0)

    def permute(l):
        step = 1024
        for j in range(LEAF // step):
            at = l * LEAF + j * step
            index = morton[:, at : at + step] - pos * BLOCK
            low = index & 255
            high = index >> 8
            hot = jnp.where(lax.broadcasted_iota(jnp.int32, (256, step), 0) == low, 1.0, 0.0).astype(BF16)
            picked = dot(folded, hot)
            total = jnp.zeros((ROWS, step), F32)
            for h in range(16):
                total = jnp.where(high == h, picked[h * ROWS : (h + 1) * ROWS], total)
            vals[0, l, :, j * step : (j + 1) * step] = total.astype(BF16)

    permute(0)
    pl.semaphore_wait(barrier, len(everyone))
    send_sel = [
        remote(sel_out.at[0], sel_in.at[1], left),
        remote(sel_out.at[1], sel_in.at[0], right),
    ]
    for copy in send_sel:
        copy.start()
    permute(1)
    for copy in send_sel:
        copy.wait_recv()

    def stage(source, target, side):
        chosen = sel_in[side, 0:1, 0:1] > 0.5
        target[side] = jnp.where(chosen, source[1].astype(F32), source[0].astype(F32)).astype(BF16)

    def halo_copies(staged, landing):
        return [remote(staged.at[0], landing.at[1], left), remote(staged.at[1], landing.at[0], right)]

    load_pts[0].wait()
    load_pts[1].wait()
    for side in range(2):
        stage(pts, stage_pts, side)
    send_pts = halo_copies(stage_pts, halo_pts)
    for copy in send_pts:
        copy.start()
    for side in range(2):
        stage(vals.at[0], stage_vals.at[0], side)
    send_vals = [halo_copies(stage_vals.at[0], halo_vals.at[0])]
    for copy in send_vals[0]:
        copy.start()

    def edges(own, landing):
        @pl.when(pos == 0)
        def _():
            landing[0] = own[0]

        @pl.when(pos == count - 1)
        def _():
            landing[1] = own[1]

    lane = lax.broadcasted_iota(jnp.int32, (HALF, 128), 1)

    def halves(first, second):
        return jnp.where(lane < 64, first, second)

    class Exchange:
        def __init__(self, prod):
            self.prod = prod

        def start(self):
            prod = self.prod
            c = [dot_nt(vals[prod, l], fr[:, l * LEAF : (l + 1) * LEAF]) for l in range(2)]
            both = c[0] + c[1]
            for h in range(2):
                coef[prod, h] = both[h * HALF : (h + 1) * HALF]
            for l in range(2):
                sib[l, :, 0:128] = c[1 - l][:, 0:128].astype(BF16)
            self.copies = [remote(coef.at[prod], p0_in.at[prod], mate)]
            self.copies[0].start()

        def spread(self, out, arrivals, axis):
            self.copies = [remote(out, arrivals.at[d], peers[axis][d]) for d in range(3)]
            for copy in self.copies:
                copy.start()

        def arrived(self):
            for copy in self.copies:
                copy.wait_recv()

        def after_core(self):
            prod = self.prod
            self.arrived()
            p1_out[prod] = coef[prod, core, :, 128:] + p0_in[prod, core, :, 128:]
            self.spread(p1_out.at[prod], p1_in.at[prod], "z")
            for l in range(2):
                for h in range(2):
                    rows = pl.ds(h * HALF, HALF)
                    sib[l, rows, 0:128] = halves(
                        sib[l, rows, 0:128].astype(F32), p0_in[prod, h, :, 0:128]
                    ).astype(BF16)

        def after_z(self):
            prod = self.prod
            self.arrived()
            a, b, c = p1_in.at[prod, 0], p1_in.at[prod, 1], p1_in.at[prod, 2]
            p2_out[prod] = (p1_out[prod, :, 128:] + a[:, 128:]) + (b[:, 128:] + c[:, 128:])
            self.spread(p2_out.at[prod], p2_in.at[prod], "x")
            sib_half[prod, core, :, 0:128] = halves(a[:, 0:128], b[:, 0:128] + c[:, 0:128]).astype(BF16)

        def after_x(self):
            prod = self.prod
            self.arrived()
            a, b, c = p2_in.at[prod, 0], p2_in.at[prod, 1], p2_in.at[prod, 2]
            p3_out[prod] = (p2_out[prod, :, 128:] + a[:, 128:]) + (b[:, 128:] + c[:, 128:])
            self.spread(p3_out.at[prod], p3_in.at[prod], "y")
            sib_half[prod, core, :, 128:256] = halves(a[:, 0:128], b[:, 0:128] + c[:, 0:128]).astype(BF16)

        def after_y(self):
            prod = self.prod
            self.arrived()
            a, b, c = p3_in[prod, 0], p3_in[prod, 1], p3_in[prod, 2]
            sib_half[prod, core, :, 256:384] = halves(a, b + c).astype(BF16)
            self.copies = [remote(sib_half.at[prod, core], sib_half.at[prod, core], mate)]
            self.copies[0].start()

        def finish(self):
            prod = self.prod
            self.arrived()
            for l in range(2):
                for h in range(2):
                    sib[l, pl.ds(h * HALF, HALF), 128:] = sib_half[prod, h]

    def prepare_source(x):
        rows = norm_rows(x, 0)
        whole = jnp.concatenate([x.astype(F32), rows, jnp.zeros((DEPTH - DIM - 8, LEAF), F32)], axis=0)
        src[...] = whole.T.astype(BF16)

    def prepare_target(l):
        x = pts[l]
        rows = norm_rows(x, 3)
        whole = jnp.concatenate(
            [x.astype(F32) * (1.0 / 16.0), rows, jnp.zeros((DEPTH - DIM - 8, LEAF), F32)], axis=0
        )
        tgt[l] = whole.astype(BF16)

    def generate(tile, l, values, part):
        at = part * 1024
        for j in range(4):
            cols = pl.ds(j * 512, 512)
            exponent = dot(src[at : at + 1024, :], tgt[l, :, cols])
            made = jnp.exp(exponent).astype(BF16)
            tiles[tile, at : at + 1024, cols] = made
            acc[l, :, cols] += dot(values[:, at : at + 1024], made)

    def apply(tile, l, values):
        acc[l] += dot(values[...], tiles[tile])

    load_fr.wait()
    first = Exchange(0)
    first.start()
    acc[...] = jnp.zeros_like(acc)
    for l in range(2):
        prepare_target(l)
    prepare_source(pts[0])
    generate(0, 0, vals.at[0, 0], 0)
    first.after_core()
    generate(0, 0, vals.at[0, 0], 1)
    prepare_source(pts[1])
    generate(1, 1, vals.at[0, 1], 0)
    first.after_z()
    generate(1, 1, vals.at[0, 1], 1)
    for copy in send_pts:
        copy.wait_recv()
    edges(pts, halo_pts)
    for copy in send_vals[0]:
        copy.wait_recv()
    edges(vals.at[0], halo_vals.at[0])
    first.after_x()
    prepare_source(halo_pts[0])
    generate(2, 0, halo_vals.at[0, 0], 0)
    generate(2, 0, halo_vals.at[0, 0], 1)
    first.after_y()
    prepare_source(halo_pts[1])
    generate(3, 1, halo_vals.at[0, 1], 0)
    generate(3, 1, halo_vals.at[0, 1], 1)
    first.finish()
    load_fl.wait()
    for l in range(2):
        whole = acc[l] + dot(sib[l], fl[:, l * LEAF : (l + 1) * LEAF])
        far_sum[l] = whole
        vals[1, l] = whole.astype(BF16)
    outs = [
        pltpu.make_async_copy(far_sum.at[l], out1.at[:, pl.ds(l * LEAF, LEAF)], out_sem.at[l]) for l in range(2)
    ]
    for copy in outs:
        copy.start()

    for side in range(2):
        stage(vals.at[1], stage_vals.at[1], side)
    send_vals.append(halo_copies(stage_vals.at[1], halo_vals.at[1]))
    for copy in send_vals[1]:
        copy.start()
    second = Exchange(1)
    second.start()
    acc[...] = jnp.zeros_like(acc)
    apply(0, 0, vals.at[1, 0])
    second.after_core()
    apply(1, 1, vals.at[1, 1])
    second.after_z()
    for copy in send_vals[1]:
        copy.wait_recv()
    edges(vals.at[1], halo_vals.at[1])
    apply(2, 0, halo_vals.at[1, 0])
    second.after_x()
    apply(3, 1, halo_vals.at[1, 1])
    second.after_y()
    second.finish()
    for l in range(2):
        acc[l] += dot(sib[l], fl[:, l * LEAF : (l + 1) * LEAF])
    more = [pltpu.make_async_copy(acc.at[l], out2.at[:, pl.ds(l * LEAF, LEAF)], out_sem.at[2 + l]) for l in range(2)]
    for copy in more:
        copy.start()
    for copy in sent:
        copy.wait_send()
    for copy in outs + more:
        copy.wait()


COPIES = 2 + 2 + 2 + 2 + 2 * (1 + 9 + 1)


def body(right_sides, morton, near_leaf, points, far_left, far_right):
    vmem = pltpu.VMEM
    hbm = pl.BlockSpec(memory_space=pl.ANY)
    out = jax.ShapeDtypeStruct((ROWS, BLOCK), F32)
    return pl.pallas_call(
        kernel,
        out_shape=(out, out),
        in_specs=[
            pl.BlockSpec(memory_space=pltpu.SMEM),
            pl.BlockSpec(memory_space=pltpu.VMEM),
            hbm, hbm, hbm, hbm,
        ],
        out_specs=(hbm, hbm),
        scratch_shapes=[
            vmem((4, LEAF, LEAF), BF16),
            vmem((WIDTH, BLOCK), BF16),
            vmem((WIDTH, BLOCK), BF16),
            vmem((2, DIM, LEAF), BF16),
            vmem((2, DIM, LEAF), BF16),
            vmem((2, DIM, LEAF), BF16),
            vmem((ROWS, BLOCK), BF16),
            vmem((2, 2, ROWS, LEAF), BF16),
            vmem((2, 2, ROWS, LEAF), BF16),
            vmem((2, 2, ROWS, LEAF), BF16),
            vmem((LEAF, DEPTH), BF16),
            vmem((2, DEPTH, LEAF), BF16),
            vmem((2, ROWS, LEAF), F32),
            vmem((2, ROWS, LEAF), F32),
            vmem((2, 8, 128), F32),
            vmem((2, 8, 128), F32),
            vmem((2, 2, HALF, WIDTH), F32),
            vmem((2, 2, HALF, WIDTH), F32),
            vmem((2, HALF, 384), F32),
            vmem((2, 3, HALF, 384), F32),
            vmem((2, HALF, 256), F32),
            vmem((2, 3, HALF, 256), F32),
            vmem((2, HALF, 128), F32),
            vmem((2, 3, HALF, 128), F32),
            vmem((2, 2, HALF, 384), BF16),
            vmem((2, ROWS, WIDTH), BF16),
            pltpu.SemaphoreType.DMA((5,)),
            pltpu.SemaphoreType.DMA((4,)),
            pltpu.SemaphoreType.DMA((COPIES,)),
            pltpu.SemaphoreType.DMA((COPIES,)),
        ],
        compiler_params=pltpu.CompilerParams(
            collective_id=0, has_side_effects=True, vmem_limit_bytes=60 << 20
        ),
    )(
        near_leaf,
        morton.reshape(1, BLOCK),
        right_sides,
        points,
        far_left.reshape(WIDTH, BLOCK),
        far_right.reshape(WIDTH, BLOCK),
    )


def solution(mesh):
    placed = (
        P("rhs", "pts"),
        P("pts"),
        P("pts"),
        P(None, "pts"),
        P(None, None, "pts"),
        P(None, None, "pts"),
    )
    return jax.shard_map(
        body,
        mesh=mesh,
        in_specs=placed,
        out_specs=(P("rhs", "pts"), P("rhs", "pts")),
        check_vma=False,
    )
```

```python
import jax
import jax.numpy as jnp
from jax import lax
from jax.experimental import pallas as pl
from jax.experimental.pallas import tpu as pltpu
from jax.sharding import PartitionSpec as P

DIM = 64
LEAF = 2048
RANK = 64
LEVELS = 8
ROWS = 32
HALF = 16
WIDTH = LEVELS * RANK
BLOCK = 2 * LEAF
DEPTH = 128
MESH = pl.DeviceIdType.MESH
F32 = jnp.float32
BF16 = jnp.bfloat16


def dot(a, b):
    return jnp.dot(a, b, preferred_element_type=F32)


def dot_nt(a, b):
    return lax.dot_general(a, b, (((1,), (1,)), ((), ())), preferred_element_type=F32)


def norm_rows(x, first):
    wide = x.astype(F32)
    a = jnp.sum(wide * wide, axis=0, keepdims=True) * (-1.0 / 32.0)
    h1 = a.astype(BF16).astype(F32)
    r1 = a - h1
    h2 = r1.astype(BF16).astype(F32)
    h3 = r1 - h2
    row = lax.broadcasted_iota(jnp.int32, (8, x.shape[1]), 0) - first
    one = jnp.where((row >= 3 - 2 * first) & (row < 6 - 2 * first), 1.0, 0.0)
    return jnp.where(row == 0, h1, jnp.where(row == 1, h2, jnp.where(row == 2, h3, one)))


def kernel(
    near, morton, rs_hbm, pts_hbm, fl_hbm, fr_hbm,
    out1, out2,
    tiles, fl, fr, pts, halo_pts, stage_pts, rs, vals, halo_vals, stage_vals,
    src, tgt, acc, far_sum, sel_out, sel_in,
    coef, p0_in, p1_sum, p1_out, p1_in, p1_out_short, p1_in_short, p2_out, p2_in, sib_low, sib_high, sib,
    local_sem, out_sem, send_sem, recv_sem,
):
    pos = lax.axis_index("pts")
    count = lax.axis_size("pts")
    core = lax.rem(pos, 2)
    mate = pos + 1 - 2 * core
    beyond = lax.rem(pos + count - 1 + 2 * core, count)
    near_slot, far_slot = 1 - core, core
    inner = jnp.logical_and(pos > 0, pos < count - 1)

    def shifted(shift, d):
        digit = lax.rem(pos // shift, 4)
        if d == 0:
            return 0
        if d == 1:
            other = digit + 1 - 2 * lax.rem(digit, 2)
        elif d == 2:
            other = lax.rem(digit + 2, 4)
        else:
            other = 3 - digit
        return (other - digit) * shift

    z_peers = [pos + shifted(2, d) for d in (1, 2, 3)]
    xy_peers = [pos + shifted(8, d % 4) + shifted(32, d // 4) for d in range(1, 16)]

    load_rs = pltpu.make_async_copy(rs_hbm, rs, local_sem.at[0])
    load_pts = [
        pltpu.make_async_copy(pts_hbm.at[:, pl.ds(l * LEAF, LEAF)], pts.at[l], local_sem.at[1 + l]) for l in range(2)
    ]
    load_fr = pltpu.make_async_copy(fr_hbm, fr, local_sem.at[3])
    load_fl = pltpu.make_async_copy(fl_hbm, fl, local_sem.at[4])
    load_rs.start()
    load_pts[0].start()
    load_pts[1].start()
    load_fr.start()
    load_fl.start()

    barrier = pltpu.get_barrier_semaphore()
    everyone = [mate, beyond] + z_peers + xy_peers
    for peer in everyone:
        pl.semaphore_signal(barrier, inc=1, device_id={"pts": peer}, device_id_type=MESH)

    slot = [0]
    sent = []

    def remote(source, target, peer, track=True):
        i = slot[0]
        slot[0] += 1
        copy = pltpu.make_async_remote_copy(
            src_ref=source, dst_ref=target, send_sem=send_sem.at[i], recv_sem=recv_sem.at[i],
            device_id={"pts": peer}, device_id_type=MESH,
        )
        if track:
            sent.append(copy)
        return copy

    class Beyond:
        def __init__(self, source, target):
            self.copy = remote(source, target, beyond, False)
            sent.append(self)

        def start(self):
            pl.when(inner)(self.copy.start)

        def wait_recv(self):
            pl.when(inner)(self.copy.wait_recv)

        def wait_send(self):
            pl.when(inner)(self.copy.wait_send)

    wanted = [near[0] - 2 * pos + 2, near[1] - 2 * pos - 2]
    sel_out[0] = jnp.full((8, 128), jnp.where(core == 0, wanted[1], wanted[0]).astype(F32))
    sel_out[1] = jnp.full((8, 128), jnp.where(core == 0, wanted[0], wanted[1]).astype(F32))

    load_rs.wait()
    folded = jnp.concatenate([rs[:, h * 256 : (h + 1) * 256] for h in range(16)], axis=0)

    def permute(l):
        step = 1024
        for j in range(LEAF // step):
            at = l * LEAF + j * step
            index = morton[:, at : at + step] - pos * BLOCK
            low = index & 255
            high = index >> 8
            hot = jnp.where(lax.broadcasted_iota(jnp.int32, (256, step), 0) == low, 1.0, 0.0).astype(BF16)
            picked = dot(folded, hot)
            total = jnp.zeros((ROWS, step), F32)
            for h in range(16):
                total = jnp.where(high == h, picked[h * ROWS : (h + 1) * ROWS], total)
            vals[0, l, :, j * step : (j + 1) * step] = total.astype(BF16)

    permute(0)
    permute(1)
    pl.semaphore_wait(barrier, len(everyone))
    sel_far = Beyond(sel_out.at[1], sel_in.at[1])
    sel_far.start()
    sel_mate = remote(sel_out.at[0], sel_in.at[0], mate)
    sel_mate.start()

    def stage(source, target, side):
        chosen = sel_in[side, 0:1, 0:1] > 0.5
        target[side] = jnp.where(chosen, source[1].astype(F32), source[0].astype(F32)).astype(BF16)

    def edges(own, landing):
        @pl.when(pos == 0)
        def _():
            landing[1] = own[0]

        @pl.when(pos == count - 1)
        def _():
            landing[1] = own[1]

    lane = lax.broadcasted_iota(jnp.int32, (HALF, 128), 1)

    def halves(first, second):
        return jnp.where(lane < 64, first, second)

    class Exchange:
        def __init__(self, prod):
            self.prod = prod

        def start(self):
            prod = self.prod
            c = [dot_nt(vals[prod, l], fr[:, l * LEAF : (l + 1) * LEAF]) for l in range(2)]
            both = c[0] + c[1]
            for h in range(2):
                coef[prod, h] = both[h * HALF : (h + 1) * HALF]
            for l in range(2):
                sib[l, :, 0:128] = c[1 - l][:, 0:128].astype(BF16)
            self.copies = [remote(coef.at[prod], p0_in.at[prod], mate)]
            self.copies[0].start()

        def arrived(self):
            for copy in self.copies:
                copy.wait_recv()

        def after_core(self):
            prod = self.prod
            self.arrived()
            p1_sum[...] = coef[prod, core, :, 128:] + p0_in[prod, core, :, 128:]
            out, arrivals = ((p1_out, p1_in), (p1_out_short, p1_in_short))[prod]
            out[...] = p1_sum[...].astype(out.dtype)
            self.copies = [remote(out, arrivals.at[d], z_peers[d]) for d in range(3)]
            for copy in self.copies:
                copy.start()
            for l in range(2):
                for h in range(2):
                    rows = pl.ds(h * HALF, HALF)
                    sib[l, rows, 0:128] = halves(
                        sib[l, rows, 0:128].astype(F32), p0_in[prod, h, :, 0:128]
                    ).astype(BF16)

        def after_z(self):
            prod = self.prod
            self.arrived()
            arrivals = (p1_in, p1_in_short)[prod]
            a, b, c = [arrivals[d].astype(F32) for d in range(3)]
            for t in range(2):
                cols = slice(128 + 128 * t, 256 + 128 * t)
                p2_out[prod, t] = (p1_sum[:, cols] + a[:, cols]) + (b[:, cols] + c[:, cols])
            self.copies = [
                remote(p2_out.at[prod, 0 if d < 4 else 1], p2_in.at[prod, d - 1], xy_peers[d - 1]) for d in range(1, 16)
            ]
            for copy in self.copies:
                copy.start()
            sib_low[prod, core] = halves(a[:, 0:128], b[:, 0:128] + c[:, 0:128]).astype(BF16)
            self.low = remote(sib_low.at[prod, core], sib_low.at[prod, core], mate)
            self.low.start()

        def after_xy(self):
            prod = self.prod
            self.arrived()

            def total(lo, hi):
                value = p2_in[prod, lo - 1]
                for d in range(lo + 1, hi):
                    value = value + p2_in[prod, d - 1]
                return value

            sib_high[prod, core, :, 0:128] = halves(total(1, 2), total(2, 4)).astype(BF16)
            sib_high[prod, core, :, 128:256] = halves(total(4, 8), total(8, 16)).astype(BF16)
            self.copies = [remote(sib_high.at[prod, core], sib_high.at[prod, core], mate)]
            self.copies[0].start()

        def finish_low(self):
            self.low.wait_recv()
            for l in range(2):
                for h in range(2):
                    sib[l, pl.ds(h * HALF, HALF), 128:256] = sib_low[self.prod, h]

        def finish_high(self):
            self.arrived()
            for l in range(2):
                for h in range(2):
                    sib[l, pl.ds(h * HALF, HALF), 256:] = sib_high[self.prod, h]

    def far(l, part):
        rows = slice(part * 256, part * 256 + 256)
        return dot(sib[l, :, rows], fl[rows, l * LEAF : (l + 1) * LEAF])

    def prepare_source(x):
        rows = norm_rows(x, 0)
        whole = jnp.concatenate([x.astype(F32), rows, jnp.zeros((DEPTH - DIM - 8, LEAF), F32)], axis=0)
        src[...] = whole.T.astype(BF16)

    def prepare_target(l):
        x = pts[l]
        rows = norm_rows(x, 3)
        whole = jnp.concatenate(
            [x.astype(F32) * (1.0 / 16.0), rows, jnp.zeros((DEPTH - DIM - 8, LEAF), F32)], axis=0
        )
        tgt[l] = whole.astype(BF16)

    def generate(tile, l, values, part):
        at = part * 1024
        for j in range(4):
            cols = pl.ds(j * 512, 512)
            exponent = dot(src[at : at + 1024, :], tgt[l, :, cols])
            made = jnp.exp(exponent).astype(BF16)
            tiles[tile, at : at + 1024, cols] = made
            acc[l, :, cols] += dot(values[:, at : at + 1024], made)

    def apply(tile, l, values, part, first=False):
        cols = pl.ds(part * 1024, 1024)
        value = dot(values[...], tiles[tile, :, cols])
        acc[l, :, cols] = value if first else acc[l, :, cols] + value

    load_fr.wait()
    first = Exchange(0)
    first.start()
    acc[...] = jnp.zeros_like(acc)
    load_pts[0].wait()
    load_pts[1].wait()
    for l in range(2):
        prepare_target(l)
    prepare_source(pts[0])
    def halo_values(prod):
        return (
            remote(stage_vals.at[prod, 0], halo_vals.at[prod, 0], mate),
            Beyond(stage_vals.at[prod, 1], halo_vals.at[prod, 1]),
        )

    sel_far.wait_recv()
    stage(pts, stage_pts, 1)
    pts_far = Beyond(stage_pts.at[1], halo_pts.at[1])
    pts_far.start()
    stage(vals.at[0], stage_vals.at[0], 1)
    vals_mate, vals_far = halo_values(0)
    vals_far.start()
    generate(0, 0, vals.at[0, 0], 0)
    first.after_core()
    sel_mate.wait_recv()
    stage(pts, stage_pts, 0)
    pts_mate = remote(stage_pts.at[0], halo_pts.at[0], mate)
    pts_mate.start()
    stage(vals.at[0], stage_vals.at[0], 0)
    vals_mate.start()
    generate(0, 0, vals.at[0, 0], 1)
    prepare_source(pts[1])
    generate(1, 1, vals.at[0, 1], 0)
    generate(1, 1, vals.at[0, 1], 1)
    pts_mate.wait_recv()
    vals_mate.wait_recv()
    first.after_z()
    prepare_source(halo_pts[0])
    generate(2, near_slot, halo_vals.at[0, 0], 0)
    generate(2, near_slot, halo_vals.at[0, 0], 1)
    load_fl.wait()
    first.finish_low()
    for l in range(2):
        acc[l] += far(l, 0)
    pts_far.wait_recv()
    edges(pts, halo_pts)
    vals_far.wait_recv()
    edges(vals.at[0], halo_vals.at[0])
    prepare_source(halo_pts[1])
    generate(3, far_slot, halo_vals.at[0, 1], 0)
    first.after_xy()
    generate(3, far_slot, halo_vals.at[0, 1], 1)
    first.finish_high()
    for l in range(2):
        whole = acc[l] + far(l, 1)
        far_sum[l] = whole
        vals[1, l] = whole.astype(BF16)
    outs = [
        pltpu.make_async_copy(far_sum.at[l], out1.at[:, pl.ds(l * LEAF, LEAF)], out_sem.at[l]) for l in range(2)
    ]
    for copy in outs:
        copy.start()

    second = Exchange(1)
    second.start()
    vals_mate, vals_far = halo_values(1)
    stage(vals.at[1], stage_vals.at[1], 0)
    vals_mate.start()
    stage(vals.at[1], stage_vals.at[1], 1)
    apply(0, 0, vals.at[1, 0], 0, True)
    second.after_core()
    vals_far.start()
    apply(0, 0, vals.at[1, 0], 1, True)
    for part in range(2):
        apply(1, 1, vals.at[1, 1], part, True)
    vals_mate.wait_recv()
    for part in range(2):
        apply(2, near_slot, halo_vals.at[1, 0], part)
    second.after_z()
    vals_far.wait_recv()
    edges(vals.at[1], halo_vals.at[1])
    for part in range(2):
        apply(3, far_slot, halo_vals.at[1, 1], part)
    second.finish_low()
    for l in range(2):
        acc[l] += far(l, 0)
    second.after_xy()
    second.finish_high()
    for l in range(2):
        acc[l] += far(l, 1)
    more = [pltpu.make_async_copy(acc.at[l], out2.at[:, pl.ds(l * LEAF, LEAF)], out_sem.at[2 + l]) for l in range(2)]
    for copy in more:
        copy.start()
    for copy in sent:
        copy.wait_send()
    for copy in outs + more:
        copy.wait()


COPIES = 2 + 2 + 2 + 2 + 2 * (1 + 3 + 15 + 2)


def copy_out(first, second, out1, out2, held, sem):
    copies = []
    for t, (source, target) in enumerate(((first, out1), (second, out2))):
        for j in range(2):
            rows = pl.ds(j * HALF, HALF)
            here = held.at[t, rows]
            copies.append((
                pltpu.make_async_copy(source.at[rows], here, sem.at[0, 2 * t + j]),
                pltpu.make_async_copy(here, target.at[rows], sem.at[1, 2 * t + j]),
            ))
    for load, _ in copies:
        load.start()
    for load, store in copies:
        load.wait()
        store.start()
    for _, store in copies:
        store.wait()


def body(right_sides, morton, near_leaf, points, far_left, far_right):
    vmem = pltpu.VMEM
    hbm = pl.BlockSpec(memory_space=pl.ANY)
    out = jax.ShapeDtypeStruct((ROWS, BLOCK), F32)
    results = pl.pallas_call(
        kernel,
        out_shape=(out, out),
        in_specs=[
            pl.BlockSpec(memory_space=pltpu.SMEM),
            pl.BlockSpec(memory_space=pltpu.VMEM),
            hbm, hbm, hbm, hbm,
        ],
        out_specs=(hbm, hbm),
        scratch_shapes=[
            vmem((4, LEAF, LEAF), BF16),
            vmem((WIDTH, BLOCK), BF16),
            vmem((WIDTH, BLOCK), BF16),
            vmem((2, DIM, LEAF), BF16),
            vmem((2, DIM, LEAF), BF16),
            vmem((2, DIM, LEAF), BF16),
            vmem((ROWS, BLOCK), BF16),
            vmem((2, 2, ROWS, LEAF), BF16),
            vmem((2, 2, ROWS, LEAF), BF16),
            vmem((2, 2, ROWS, LEAF), BF16),
            vmem((LEAF, DEPTH), BF16),
            vmem((2, DEPTH, LEAF), BF16),
            vmem((2, ROWS, LEAF), F32),
            vmem((2, ROWS, LEAF), F32),
            vmem((2, 8, 128), F32),
            vmem((2, 8, 128), F32),
            vmem((2, 2, HALF, WIDTH), F32),
            vmem((2, 2, HALF, WIDTH), F32),
            vmem((HALF, 384), F32),
            vmem((HALF, 384), F32),
            vmem((3, HALF, 384), F32),
            vmem((HALF, 384), BF16),
            vmem((3, HALF, 384), BF16),
            vmem((2, 2, HALF, 128), F32),
            vmem((2, 15, HALF, 128), F32),
            vmem((2, 2, HALF, 128), BF16),
            vmem((2, 2, HALF, 256), BF16),
            vmem((2, ROWS, WIDTH), BF16),
            pltpu.SemaphoreType.DMA((5,)),
            pltpu.SemaphoreType.DMA((4,)),
            pltpu.SemaphoreType.DMA((COPIES,)),
            pltpu.SemaphoreType.DMA((COPIES,)),
        ],
        compiler_params=pltpu.CompilerParams(
            collective_id=0, has_side_effects=True, vmem_limit_bytes=60 << 20
        ),
    )(
        near_leaf,
        morton.reshape(1, BLOCK),
        right_sides,
        points,
        far_left.reshape(WIDTH, BLOCK),
        far_right.reshape(WIDTH, BLOCK),
    )
    return pl.pallas_call(
        copy_out,
        out_shape=(out, out),
        in_specs=[hbm, hbm],
        out_specs=(hbm, hbm),
        scratch_shapes=[pltpu.VMEM((2, ROWS, BLOCK), F32), pltpu.SemaphoreType.DMA((2, 4))],
    )(*results)


def solution(mesh):
    placed = (
        P("rhs", "pts"),
        P("pts"),
        P("pts"),
        P(None, "pts"),
        P(None, None, "pts"),
        P(None, None, "pts"),
    )
    return jax.shard_map(
        body,
        mesh=mesh,
        in_specs=placed,
        out_specs=(P("rhs", "pts"), P("rhs", "pts")),
        check_vma=False,
    )
```

```python
import jax
import jax.numpy as jnp
from jax import lax
from jax.experimental import pallas as pl
from jax.experimental.pallas import tpu as pltpu
from jax.sharding import PartitionSpec as P

DIM = 64
LEAF = 2048
RANK = 64
LEVELS = 8
ROWS = 32
HALF = 16
WIDTH = LEVELS * RANK
BLOCK = 2 * LEAF
DEPTH = 128
MESH = pl.DeviceIdType.MESH
F32 = jnp.float32
BF16 = jnp.bfloat16


def dot(a, b):
    return jnp.dot(a, b, preferred_element_type=F32)


def dot_nt(a, b):
    return lax.dot_general(a, b, (((1,), (1,)), ((), ())), preferred_element_type=F32)


def norm_rows(x, first):
    wide = x.astype(F32)
    a = jnp.sum(wide * wide, axis=0, keepdims=True) * (-1.0 / 32.0)
    h1 = a.astype(BF16).astype(F32)
    r1 = a - h1
    h2 = r1.astype(BF16).astype(F32)
    h3 = r1 - h2
    row = lax.broadcasted_iota(jnp.int32, (8, x.shape[1]), 0) - first
    one = jnp.where((row >= 3 - 2 * first) & (row < 6 - 2 * first), 1.0, 0.0)
    return jnp.where(row == 0, h1, jnp.where(row == 1, h2, jnp.where(row == 2, h3, one)))


def kernel(
    near, morton, rs_hbm, pts_hbm, fl_hbm, fr_hbm,
    out1, out2,
    tiles, fl, fr, pts, halo_pts, stage_pts, rs, vals, halo_vals, stage_vals,
    src, tgt, acc, far_sum, sel_out, sel_in,
    coef, p0_in, p1_sum, p1_out, p1_in, p1_out_short, p1_in_short, p2_out, p2_in, sib_low, sib_high, sib,
    local_sem, out_sem, send_sem, recv_sem,
):
    pos = lax.axis_index("pts")
    count = lax.axis_size("pts")
    core = lax.rem(pos, 2)
    mate = pos + 1 - 2 * core
    beyond = lax.rem(pos + count - 1 + 2 * core, count)
    near_slot, far_slot = 1 - core, core
    inner = jnp.logical_and(pos > 0, pos < count - 1)

    def shifted(shift, d):
        digit = lax.rem(pos // shift, 4)
        if d == 0:
            return 0
        if d == 1:
            other = digit + 1 - 2 * lax.rem(digit, 2)
        elif d == 2:
            other = lax.rem(digit + 2, 4)
        else:
            other = 3 - digit
        return (other - digit) * shift

    z_peers = [pos + shifted(2, d) for d in (1, 2, 3)]
    xy_peers = [pos + shifted(8, d % 4) + shifted(32, d // 4) for d in range(1, 16)]

    load_rs = pltpu.make_async_copy(rs_hbm, rs, local_sem.at[0])
    load_pts = [
        pltpu.make_async_copy(pts_hbm.at[:, pl.ds(l * LEAF, LEAF)], pts.at[l], local_sem.at[1 + l]) for l in range(2)
    ]
    load_fr = pltpu.make_async_copy(fr_hbm, fr, local_sem.at[3])
    load_fl = pltpu.make_async_copy(fl_hbm, fl, local_sem.at[4])
    load_rs.start()
    load_pts[0].start()
    load_pts[1].start()
    load_fr.start()
    load_fl.start()

    barrier = pltpu.get_barrier_semaphore()
    everyone = [mate, beyond] + z_peers + xy_peers
    for peer in everyone:
        pl.semaphore_signal(barrier, inc=1, device_id={"pts": peer}, device_id_type=MESH)

    slot = [0]
    sent = []

    def remote(source, target, peer, track=True):
        i = slot[0]
        slot[0] += 1
        copy = pltpu.make_async_remote_copy(
            src_ref=source, dst_ref=target, send_sem=send_sem.at[i], recv_sem=recv_sem.at[i],
            device_id={"pts": peer}, device_id_type=MESH,
        )
        if track:
            sent.append(copy)
        return copy

    class Beyond:
        def __init__(self, source, target):
            self.copy = remote(source, target, beyond, False)
            sent.append(self)

        def start(self):
            pl.when(inner)(self.copy.start)

        def wait_recv(self):
            pl.when(inner)(self.copy.wait_recv)

        def wait_send(self):
            pl.when(inner)(self.copy.wait_send)

    wanted = [near[0] - 2 * pos + 2, near[1] - 2 * pos - 2]
    sel_out[0] = jnp.full((8, 128), jnp.where(core == 0, wanted[1], wanted[0]).astype(F32))
    sel_out[1] = jnp.full((8, 128), jnp.where(core == 0, wanted[0], wanted[1]).astype(F32))

    pl.semaphore_wait(barrier, len(everyone))
    sel_far = Beyond(sel_out.at[1], sel_in.at[1])
    sel_far.start()
    sel_mate = remote(sel_out.at[0], sel_in.at[0], mate)
    sel_mate.start()

    load_rs.wait()
    folded = jnp.concatenate([rs[:, h * 256 : (h + 1) * 256] for h in range(16)], axis=0)

    def permute(l):
        step = 1024
        for j in range(LEAF // step):
            at = l * LEAF + j * step
            index = morton[:, at : at + step] - pos * BLOCK
            low = index & 255
            high = index >> 8
            hot = jnp.where(lax.broadcasted_iota(jnp.int32, (256, step), 0) == low, 1.0, 0.0).astype(BF16)
            picked = dot(folded, hot)
            total = jnp.zeros((ROWS, step), F32)
            for h in range(16):
                total = jnp.where(high == h, picked[h * ROWS : (h + 1) * ROWS], total)
            vals[0, l, :, j * step : (j + 1) * step] = total.astype(BF16)

    permute(0)
    permute(1)
    def stage(source, target, side):
        chosen = sel_in[side, 0:1, 0:1] > 0.5
        target[side] = jnp.where(chosen, source[1].astype(F32), source[0].astype(F32)).astype(BF16)

    def edges(own, landing):
        @pl.when(pos == 0)
        def _():
            landing[1] = own[0]

        @pl.when(pos == count - 1)
        def _():
            landing[1] = own[1]

    lane = lax.broadcasted_iota(jnp.int32, (HALF, 128), 1)

    def halves(first, second):
        return jnp.where(lane < 64, first, second)

    class Exchange:
        def __init__(self, prod):
            self.prod = prod

        def start(self):
            prod = self.prod
            c = [dot_nt(vals[prod, l], fr[:, l * LEAF : (l + 1) * LEAF]) for l in range(2)]
            both = c[0] + c[1]
            for h in range(2):
                coef[prod, h] = both[h * HALF : (h + 1) * HALF]
            self.copies = [remote(coef.at[prod], p0_in.at[prod], mate)]
            self.copies[0].start()
            for l in range(2):
                sib[l, :, 0:128] = c[1 - l][:, 0:128].astype(BF16)

        def arrived(self):
            for copy in self.copies:
                copy.wait_recv()

        def after_core(self):
            prod = self.prod
            self.arrived()
            p1_sum[...] = coef[prod, core, :, 128:] + p0_in[prod, core, :, 128:]
            out, arrivals = ((p1_out, p1_in), (p1_out_short, p1_in_short))[prod]
            out[...] = p1_sum[...].astype(out.dtype)
            self.copies = [remote(out, arrivals.at[d], z_peers[d]) for d in range(3)]
            for copy in self.copies:
                copy.start()
            for l in range(2):
                for h in range(2):
                    rows = pl.ds(h * HALF, HALF)
                    sib[l, rows, 0:128] = halves(
                        sib[l, rows, 0:128].astype(F32), p0_in[prod, h, :, 0:128]
                    ).astype(BF16)

        def after_z(self):
            prod = self.prod
            self.arrived()
            arrivals = (p1_in, p1_in_short)[prod]
            a, b, c = [arrivals[d].astype(F32) for d in range(3)]
            for t in range(2):
                cols = slice(128 + 128 * t, 256 + 128 * t)
                p2_out[prod, t] = (p1_sum[:, cols] + a[:, cols]) + (b[:, cols] + c[:, cols])
            self.copies = [
                remote(p2_out.at[prod, 0 if d < 4 else 1], p2_in.at[prod, d - 1], xy_peers[d - 1]) for d in range(1, 16)
            ]
            for copy in self.copies:
                copy.start()
            sib_low[prod, core] = halves(a[:, 0:128], b[:, 0:128] + c[:, 0:128]).astype(BF16)
            self.low = remote(sib_low.at[prod, core], sib_low.at[prod, core], mate)
            self.low.start()

        def after_xy(self):
            prod = self.prod
            self.arrived()

            def total(lo, hi):
                value = p2_in[prod, lo - 1]
                for d in range(lo + 1, hi):
                    value = value + p2_in[prod, d - 1]
                return value

            sib_high[prod, core, :, 0:128] = halves(total(1, 2), total(2, 4)).astype(BF16)
            sib_high[prod, core, :, 128:256] = halves(total(4, 8), total(8, 16)).astype(BF16)
            self.copies = [remote(sib_high.at[prod, core], sib_high.at[prod, core], mate)]
            self.copies[0].start()

        def finish_low(self):
            self.low.wait_recv()
            for l in range(2):
                for h in range(2):
                    sib[l, pl.ds(h * HALF, HALF), 128:256] = sib_low[self.prod, h]

        def finish_high(self):
            self.arrived()
            for l in range(2):
                for h in range(2):
                    sib[l, pl.ds(h * HALF, HALF), 256:] = sib_high[self.prod, h]

    def far(l, part):
        rows = slice(part * 256, part * 256 + 256)
        return dot(sib[l, :, rows], fl[rows, l * LEAF : (l + 1) * LEAF])

    def prepare_source(x):
        rows = norm_rows(x, 0)
        whole = jnp.concatenate([x.astype(F32), rows, jnp.zeros((DEPTH - DIM - 8, LEAF), F32)], axis=0)
        src[...] = whole.T.astype(BF16)

    def prepare_target(l):
        x = pts[l]
        rows = norm_rows(x, 3)
        whole = jnp.concatenate(
            [x.astype(F32) * (1.0 / 16.0), rows, jnp.zeros((DEPTH - DIM - 8, LEAF), F32)], axis=0
        )
        tgt[l] = whole.astype(BF16)

    def generate(tile, l, values, part):
        at = part * 1024
        for j in range(4):
            cols = pl.ds(j * 512, 512)
            exponent = dot(src[at : at + 1024, :], tgt[l, :, cols])
            made = jnp.exp(exponent).astype(BF16)
            tiles[tile, at : at + 1024, cols] = made
            acc[l, :, cols] += dot(values[:, at : at + 1024], made)

    def apply(tile, l, values, part, first=False):
        cols = pl.ds(part * 1024, 1024)
        value = dot(values[...], tiles[tile, :, cols])
        acc[l, :, cols] = value if first else acc[l, :, cols] + value

    load_pts[0].wait()
    load_pts[1].wait()
    def halo_values(prod):
        return (
            remote(stage_vals.at[prod, 0], halo_vals.at[prod, 0], mate),
            Beyond(stage_vals.at[prod, 1], halo_vals.at[prod, 1]),
        )

    load_fr.wait()
    first = Exchange(0)
    first.start()
    acc[...] = jnp.zeros_like(acc)
    for l in range(2):
        prepare_target(l)
    prepare_source(pts[0])
    sel_far.wait_recv()
    stage(pts, stage_pts, 1)
    stage(vals.at[0], stage_vals.at[0], 1)
    first.after_core()
    pts_far = Beyond(stage_pts.at[1], halo_pts.at[1])
    pts_far.start()
    vals_mate, vals_far = halo_values(0)
    vals_far.start()
    generate(0, 0, vals.at[0, 0], 0)
    sel_mate.wait_recv()
    stage(pts, stage_pts, 0)
    pts_mate = remote(stage_pts.at[0], halo_pts.at[0], mate)
    pts_mate.start()
    stage(vals.at[0], stage_vals.at[0], 0)
    vals_mate.start()
    generate(0, 0, vals.at[0, 0], 1)
    prepare_source(pts[1])
    generate(1, 1, vals.at[0, 1], 0)
    generate(1, 1, vals.at[0, 1], 1)
    pts_mate.wait_recv()
    vals_mate.wait_recv()
    first.after_z()
    prepare_source(halo_pts[0])
    generate(2, near_slot, halo_vals.at[0, 0], 0)
    generate(2, near_slot, halo_vals.at[0, 0], 1)
    pts_far.wait_recv()
    edges(pts, halo_pts)
    vals_far.wait_recv()
    edges(vals.at[0], halo_vals.at[0])
    prepare_source(halo_pts[1])
    generate(3, far_slot, halo_vals.at[0, 1], 0)
    load_fl.wait()
    first.finish_low()
    for l in range(2):
        acc[l] += far(l, 0)
    first.after_xy()
    generate(3, far_slot, halo_vals.at[0, 1], 1)
    first.finish_high()
    for l in range(2):
        whole = acc[l] + far(l, 1)
        far_sum[l] = whole
        vals[1, l] = whole.astype(BF16)
    outs = [
        pltpu.make_async_copy(far_sum.at[l], out1.at[:, pl.ds(l * LEAF, LEAF)], out_sem.at[l]) for l in range(2)
    ]
    for copy in outs:
        copy.start()

    vals_mate, vals_far = halo_values(1)
    stage(vals.at[1], stage_vals.at[1], 1)
    vals_far.start()
    second = Exchange(1)
    second.start()
    stage(vals.at[1], stage_vals.at[1], 0)
    vals_mate.start()
    apply(0, 0, vals.at[1, 0], 0, True)
    second.after_core()
    apply(0, 0, vals.at[1, 0], 1, True)
    for part in range(2):
        apply(1, 1, vals.at[1, 1], part, True)
    vals_mate.wait_recv()
    for part in range(2):
        apply(2, near_slot, halo_vals.at[1, 0], part)
    second.after_z()
    vals_far.wait_recv()
    edges(vals.at[1], halo_vals.at[1])
    for part in range(2):
        apply(3, far_slot, halo_vals.at[1, 1], part)
    second.finish_low()
    for l in range(2):
        acc[l] += far(l, 0)
    second.after_xy()
    second.finish_high()
    for l in range(2):
        acc[l] += far(l, 1)
    more = [pltpu.make_async_copy(acc.at[l], out2.at[:, pl.ds(l * LEAF, LEAF)], out_sem.at[2 + l]) for l in range(2)]
    for copy in more:
        copy.start()
    for copy in sent:
        copy.wait_send()
    for copy in outs + more:
        copy.wait()


COPIES = 2 + 2 + 2 + 2 + 2 * (1 + 3 + 15 + 2)


def copy_out(first, second, out1, out2, held, sem):
    copies = []
    for t, (source, target) in enumerate(((first, out1), (second, out2))):
        for j in range(2):
            rows = pl.ds(j * HALF, HALF)
            here = held.at[t, rows]
            copies.append((
                pltpu.make_async_copy(source.at[rows], here, sem.at[0, 2 * t + j]),
                pltpu.make_async_copy(here, target.at[rows], sem.at[1, 2 * t + j]),
            ))
    for load, _ in copies:
        load.start()
    for load, store in copies:
        load.wait()
        store.start()
    for _, store in copies:
        store.wait()


def body(right_sides, morton, near_leaf, points, far_left, far_right):
    vmem = pltpu.VMEM
    hbm = pl.BlockSpec(memory_space=pl.ANY)
    out = jax.ShapeDtypeStruct((ROWS, BLOCK), F32)
    results = pl.pallas_call(
        kernel,
        out_shape=(out, out),
        in_specs=[
            pl.BlockSpec(memory_space=pltpu.SMEM),
            pl.BlockSpec(memory_space=pltpu.VMEM),
            hbm, hbm, hbm, hbm,
        ],
        out_specs=(hbm, hbm),
        scratch_shapes=[
            vmem((4, LEAF, LEAF), BF16),
            vmem((WIDTH, BLOCK), BF16),
            vmem((WIDTH, BLOCK), BF16),
            vmem((2, DIM, LEAF), BF16),
            vmem((2, DIM, LEAF), BF16),
            vmem((2, DIM, LEAF), BF16),
            vmem((ROWS, BLOCK), BF16),
            vmem((2, 2, ROWS, LEAF), BF16),
            vmem((2, 2, ROWS, LEAF), BF16),
            vmem((2, 2, ROWS, LEAF), BF16),
            vmem((LEAF, DEPTH), BF16),
            vmem((2, DEPTH, LEAF), BF16),
            vmem((2, ROWS, LEAF), F32),
            vmem((2, ROWS, LEAF), F32),
            vmem((2, 8, 128), F32),
            vmem((2, 8, 128), F32),
            vmem((2, 2, HALF, WIDTH), F32),
            vmem((2, 2, HALF, WIDTH), F32),
            vmem((HALF, 384), F32),
            vmem((HALF, 384), F32),
            vmem((3, HALF, 384), F32),
            vmem((HALF, 384), BF16),
            vmem((3, HALF, 384), BF16),
            vmem((2, 2, HALF, 128), F32),
            vmem((2, 15, HALF, 128), F32),
            vmem((2, 2, HALF, 128), BF16),
            vmem((2, 2, HALF, 256), BF16),
            vmem((2, ROWS, WIDTH), BF16),
            pltpu.SemaphoreType.DMA((5,)),
            pltpu.SemaphoreType.DMA((4,)),
            pltpu.SemaphoreType.DMA((COPIES,)),
            pltpu.SemaphoreType.DMA((COPIES,)),
        ],
        compiler_params=pltpu.CompilerParams(
            collective_id=0, has_side_effects=True, vmem_limit_bytes=60 << 20
        ),
    )(
        near_leaf,
        morton.reshape(1, BLOCK),
        right_sides,
        points,
        far_left.reshape(WIDTH, BLOCK),
        far_right.reshape(WIDTH, BLOCK),
    )
    return pl.pallas_call(
        copy_out,
        out_shape=(out, out),
        in_specs=[hbm, hbm],
        out_specs=(hbm, hbm),
        scratch_shapes=[pltpu.VMEM((2, ROWS, BLOCK), F32), pltpu.SemaphoreType.DMA((2, 4))],
    )(*results)


def solution(mesh):
    placed = (
        P("rhs", "pts"),
        P("pts"),
        P("pts"),
        P(None, "pts"),
        P(None, None, "pts"),
        P(None, None, "pts"),
    )
    return jax.shard_map(
        body,
        mesh=mesh,
        in_specs=placed,
        out_specs=(P("rhs", "pts"), P("rhs", "pts")),
        check_vma=False,
    )
```

```python
import jax
import jax.numpy as jnp
from jax import lax
from jax.experimental import pallas as pl
from jax.experimental.pallas import tpu as pltpu
from jax.sharding import PartitionSpec as P

DIM = 64
LEAF = 2048
RANK = 64
LEVELS = 8
ROWS = 32
HALF = 16
WIDTH = LEVELS * RANK
BLOCK = 2 * LEAF
DEPTH = 128
MESH = pl.DeviceIdType.MESH
F32 = jnp.float32
BF16 = jnp.bfloat16


def dot(a, b):
    return jnp.dot(a, b, preferred_element_type=F32)


def dot_nt(a, b):
    return lax.dot_general(a, b, (((1,), (1,)), ((), ())), preferred_element_type=F32)


def norm_rows(x, first):
    wide = x.astype(F32)
    a = jnp.sum(wide * wide, axis=0, keepdims=True) * (-1.0 / 32.0)
    h1 = a.astype(BF16).astype(F32)
    r1 = a - h1
    h2 = r1.astype(BF16).astype(F32)
    h3 = r1 - h2
    row = lax.broadcasted_iota(jnp.int32, (8, x.shape[1]), 0) - first
    one = jnp.where((row >= 3 - 2 * first) & (row < 6 - 2 * first), 1.0, 0.0)
    return jnp.where(row == 0, h1, jnp.where(row == 1, h2, jnp.where(row == 2, h3, one)))


def kernel(
    near, morton, rs_hbm, pts_hbm, fl_hbm, fr_hbm,
    out1, out2,
    tiles, fl, fr, pts, halo_pts, stage_pts, rs, vals, halo_vals, stage_vals,
    src, tgt, acc, far_sum, sel_out, sel_in,
    coef, p0_in, p1_sum, p1_out, p1_in, p1_out_short, p1_in_short, p2_out, p2_in, sib_low, sib_high, sib,
    local_sem, out_sem, send_sem, recv_sem,
):
    pos = lax.axis_index("pts")
    count = lax.axis_size("pts")
    core = lax.rem(pos, 2)
    mate = pos + 1 - 2 * core
    beyond = lax.rem(pos + count - 1 + 2 * core, count)
    near_slot, far_slot = 1 - core, core
    inner = jnp.logical_and(pos > 0, pos < count - 1)

    def shifted(shift, d):
        digit = lax.rem(pos // shift, 4)
        if d == 0:
            return 0
        if d == 1:
            other = digit + 1 - 2 * lax.rem(digit, 2)
        elif d == 2:
            other = lax.rem(digit + 2, 4)
        else:
            other = 3 - digit
        return (other - digit) * shift

    z_peers = [pos + shifted(2, d) for d in (1, 2, 3)]
    xy_peers = [pos + shifted(8, d % 4) + shifted(32, d // 4) for d in range(1, 16)]

    load_rs = pltpu.make_async_copy(rs_hbm, rs, local_sem.at[0])
    load_pts = [
        pltpu.make_async_copy(pts_hbm.at[:, pl.ds(l * LEAF, LEAF)], pts.at[l], local_sem.at[1 + l]) for l in range(2)
    ]
    load_fr = pltpu.make_async_copy(fr_hbm, fr, local_sem.at[3])
    load_fl = pltpu.make_async_copy(fl_hbm, fl, local_sem.at[4])
    load_rs.start()
    load_pts[0].start()
    load_pts[1].start()
    load_fr.start()
    load_fl.start()

    barrier = pltpu.get_barrier_semaphore()
    everyone = [mate, beyond] + z_peers + xy_peers
    for peer in everyone:
        pl.semaphore_signal(barrier, inc=1, device_id={"pts": peer}, device_id_type=MESH)

    slot = [0]
    sent = []

    def remote(source, target, peer, track=True):
        i = slot[0]
        slot[0] += 1
        copy = pltpu.make_async_remote_copy(
            src_ref=source, dst_ref=target, send_sem=send_sem.at[i], recv_sem=recv_sem.at[i],
            device_id={"pts": peer}, device_id_type=MESH,
        )
        if track:
            sent.append(copy)
        return copy

    class Beyond:
        def __init__(self, source, target):
            self.copy = remote(source, target, beyond, False)
            sent.append(self)

        def start(self):
            pl.when(inner)(self.copy.start)

        def wait_recv(self):
            pl.when(inner)(self.copy.wait_recv)

        def wait_send(self):
            pl.when(inner)(self.copy.wait_send)

    wanted = [near[0] - 2 * pos + 2, near[1] - 2 * pos - 2]
    sel_out[0] = jnp.full((8, 128), jnp.where(core == 0, wanted[1], wanted[0]).astype(F32))
    sel_out[1] = jnp.full((8, 128), jnp.where(core == 0, wanted[0], wanted[1]).astype(F32))

    pl.semaphore_wait(barrier, len(everyone))
    sel_far = Beyond(sel_out.at[1], sel_in.at[1])
    sel_far.start()
    sel_mate = remote(sel_out.at[0], sel_in.at[0], mate)
    sel_mate.start()

    load_rs.wait()
    folded = jnp.concatenate([rs[:, h * 256 : (h + 1) * 256] for h in range(16)], axis=0)

    def permute(l):
        step = 1024
        for j in range(LEAF // step):
            at = l * LEAF + j * step
            index = morton[:, at : at + step] - pos * BLOCK
            low = index & 255
            high = index >> 8
            hot = jnp.where(lax.broadcasted_iota(jnp.int32, (256, step), 0) == low, 1.0, 0.0).astype(BF16)
            picked = dot(folded, hot)
            total = jnp.zeros((ROWS, step), F32)
            for h in range(16):
                total = jnp.where(high == h, picked[h * ROWS : (h + 1) * ROWS], total)
            vals[0, l, :, j * step : (j + 1) * step] = total.astype(BF16)

    permute(0)
    permute(1)
    def stage(source, target, side):
        chosen = sel_in[side, 0:1, 0:1] > 0.5
        target[side] = jnp.where(chosen, source[1].astype(F32), source[0].astype(F32)).astype(BF16)

    def edges(own, landing):
        @pl.when(pos == 0)
        def _():
            landing[1] = own[0]

        @pl.when(pos == count - 1)
        def _():
            landing[1] = own[1]

    lane = lax.broadcasted_iota(jnp.int32, (HALF, 128), 1)

    def halves(first, second):
        return jnp.where(lane < 64, first, second)

    class Exchange:
        def __init__(self, prod):
            self.prod = prod

        def start(self):
            prod = self.prod
            c = [dot_nt(vals[prod, l], fr[:, l * LEAF : (l + 1) * LEAF]) for l in range(2)]
            both = c[0] + c[1]
            for h in range(2):
                coef[prod, h] = both[h * HALF : (h + 1) * HALF]
            self.copies = [remote(coef.at[prod], p0_in.at[prod], mate)]
            self.copies[0].start()
            for l in range(2):
                sib[l, :, 0:128] = c[1 - l][:, 0:128].astype(BF16)

        def arrived(self):
            for copy in self.copies:
                copy.wait_recv()

        def after_core(self):
            prod = self.prod
            self.arrived()
            p1_sum[...] = coef[prod, core, :, 128:] + p0_in[prod, core, :, 128:]
            out, arrivals = ((p1_out, p1_in), (p1_out_short, p1_in_short))[prod]
            out[...] = p1_sum[...].astype(out.dtype)
            self.copies = [remote(out, arrivals.at[d], z_peers[d]) for d in range(3)]
            for copy in self.copies:
                copy.start()
            for l in range(2):
                for h in range(2):
                    rows = pl.ds(h * HALF, HALF)
                    sib[l, rows, 0:128] = halves(
                        sib[l, rows, 0:128].astype(F32), p0_in[prod, h, :, 0:128]
                    ).astype(BF16)

        def after_z(self):
            prod = self.prod
            self.arrived()
            arrivals = (p1_in, p1_in_short)[prod]
            a, b, c = [arrivals[d].astype(F32) for d in range(3)]
            for t in range(2):
                cols = slice(128 + 128 * t, 256 + 128 * t)
                p2_out[prod, t] = (p1_sum[:, cols] + a[:, cols]) + (b[:, cols] + c[:, cols])
            self.copies = [
                remote(p2_out.at[prod, 0 if d < 4 else 1], p2_in.at[prod, d - 1], xy_peers[d - 1]) for d in range(1, 16)
            ]
            for copy in self.copies:
                copy.start()
            sib_low[prod, core] = halves(a[:, 0:128], b[:, 0:128] + c[:, 0:128]).astype(BF16)
            self.low = remote(sib_low.at[prod, core], sib_low.at[prod, core], mate)
            self.low.start()

        def after_xy(self):
            prod = self.prod
            self.arrived()

            def total(lo, hi):
                value = p2_in[prod, lo - 1]
                for d in range(lo + 1, hi):
                    value = value + p2_in[prod, d - 1]
                return value

            sib_high[prod, core, :, 0:128] = halves(total(1, 2), total(2, 4)).astype(BF16)
            sib_high[prod, core, :, 128:256] = halves(total(4, 8), total(8, 16)).astype(BF16)
            self.copies = [remote(sib_high.at[prod, core], sib_high.at[prod, core], mate)]
            self.copies[0].start()

        def finish_low(self):
            self.low.wait_recv()
            for l in range(2):
                for h in range(2):
                    sib[l, pl.ds(h * HALF, HALF), 128:256] = sib_low[self.prod, h]

        def finish_high(self):
            self.arrived()
            for l in range(2):
                for h in range(2):
                    sib[l, pl.ds(h * HALF, HALF), 256:] = sib_high[self.prod, h]

    def far(l, part):
        rows = slice(part * 256, part * 256 + 256)
        return dot(sib[l, :, rows], fl[rows, l * LEAF : (l + 1) * LEAF])

    def prepare_source(x):
        rows = norm_rows(x, 0)
        whole = jnp.concatenate([x.astype(F32), rows, jnp.zeros((DEPTH - DIM - 8, LEAF), F32)], axis=0)
        src[...] = whole.T.astype(BF16)

    def prepare_target(l):
        x = pts[l]
        rows = norm_rows(x, 3)
        whole = jnp.concatenate(
            [x.astype(F32) * (1.0 / 16.0), rows, jnp.zeros((DEPTH - DIM - 8, LEAF), F32)], axis=0
        )
        tgt[l] = whole.astype(BF16)

    def generate(tile, l, values, part):
        at = part * 1024
        for j in range(4):
            cols = pl.ds(j * 512, 512)
            exponent = dot(src[at : at + 1024, :], tgt[l, :, cols])
            made = jnp.exp(exponent).astype(BF16)
            tiles[tile, at : at + 1024, cols] = made
            acc[l, :, cols] += dot(values[:, at : at + 1024], made)

    def apply(tile, l, values, part, first=False):
        cols = pl.ds(part * 1024, 1024)
        value = dot(values[...], tiles[tile, :, cols])
        acc[l, :, cols] = value if first else acc[l, :, cols] + value

    load_pts[0].wait()
    load_pts[1].wait()
    def halo_values(prod):
        return (
            remote(stage_vals.at[prod, 0], halo_vals.at[prod, 0], mate),
            Beyond(stage_vals.at[prod, 1], halo_vals.at[prod, 1]),
        )

    load_fr.wait()
    first = Exchange(0)
    first.start()
    acc[...] = jnp.zeros_like(acc)
    for l in range(2):
        prepare_target(l)
    prepare_source(pts[0])
    sel_far.wait_recv()
    stage(pts, stage_pts, 1)
    stage(vals.at[0], stage_vals.at[0], 1)
    first.after_core()
    pts_far = Beyond(stage_pts.at[1], halo_pts.at[1])
    pts_far.start()
    vals_mate, vals_far = halo_values(0)
    vals_far.start()
    generate(0, 0, vals.at[0, 0], 0)
    sel_mate.wait_recv()
    stage(pts, stage_pts, 0)
    pts_mate = remote(stage_pts.at[0], halo_pts.at[0], mate)
    pts_mate.start()
    stage(vals.at[0], stage_vals.at[0], 0)
    vals_mate.start()
    generate(0, 0, vals.at[0, 0], 1)
    prepare_source(pts[1])
    generate(1, 1, vals.at[0, 1], 0)
    generate(1, 1, vals.at[0, 1], 1)
    pts_mate.wait_recv()
    vals_mate.wait_recv()
    first.after_z()
    prepare_source(halo_pts[0])
    generate(2, near_slot, halo_vals.at[0, 0], 0)
    generate(2, near_slot, halo_vals.at[0, 0], 1)
    pts_far.wait_recv()
    edges(pts, halo_pts)
    vals_far.wait_recv()
    edges(vals.at[0], halo_vals.at[0])
    prepare_source(halo_pts[1])
    generate(3, far_slot, halo_vals.at[0, 1], 0)
    load_fl.wait()
    first.finish_low()
    for l in range(2):
        acc[l] += far(l, 0)
    first.after_xy()
    generate(3, far_slot, halo_vals.at[0, 1], 1)
    first.finish_high()
    for l in range(2):
        whole = acc[l] + far(l, 1)
        far_sum[l] = whole
        vals[1, l] = whole.astype(BF16)
    outs = [
        pltpu.make_async_copy(far_sum.at[l], out1.at[:, pl.ds(l * LEAF, LEAF)], out_sem.at[l]) for l in range(2)
    ]
    for copy in outs:
        copy.start()

    vals_mate, vals_far = halo_values(1)
    stage(vals.at[1], stage_vals.at[1], 1)
    vals_far.start()
    second = Exchange(1)
    second.start()
    stage(vals.at[1], stage_vals.at[1], 0)
    vals_mate.start()
    apply(0, 0, vals.at[1, 0], 0, True)
    second.after_core()
    apply(0, 0, vals.at[1, 0], 1, True)
    for part in range(2):
        apply(1, 1, vals.at[1, 1], part, True)
    vals_mate.wait_recv()
    apply(2, near_slot, halo_vals.at[1, 0], 0)
    second.after_z()
    apply(2, near_slot, halo_vals.at[1, 0], 1)
    vals_far.wait_recv()
    edges(vals.at[1], halo_vals.at[1])
    for part in range(2):
        apply(3, far_slot, halo_vals.at[1, 1], part)
    second.finish_low()
    for l in range(2):
        acc[l] += far(l, 0)
    second.after_xy()
    second.finish_high()
    more = [pltpu.make_async_copy(acc.at[l], out2.at[:, pl.ds(l * LEAF, LEAF)], out_sem.at[2 + l]) for l in range(2)]
    for l in range(2):
        acc[l] += far(l, 1)
        more[l].start()
    for copy in sent:
        copy.wait_send()
    for copy in outs + more:
        copy.wait()


COPIES = 2 + 2 + 2 + 2 + 2 * (1 + 3 + 15 + 2)


def copy_out(first, second, out1, out2, held, sem):
    copies = []
    for t, (source, target) in enumerate(((first, out1), (second, out2))):
        for j in range(2):
            rows = pl.ds(j * HALF, HALF)
            here = held.at[t, rows]
            copies.append((
                pltpu.make_async_copy(source.at[rows], here, sem.at[0, 2 * t + j]),
                pltpu.make_async_copy(here, target.at[rows], sem.at[1, 2 * t + j]),
            ))
    for load, _ in copies:
        load.start()
    for load, store in copies:
        load.wait()
        store.start()
    for _, store in copies:
        store.wait()


def body(right_sides, morton, near_leaf, points, far_left, far_right):
    vmem = pltpu.VMEM
    hbm = pl.BlockSpec(memory_space=pl.ANY)
    out = jax.ShapeDtypeStruct((ROWS, BLOCK), F32)
    results = pl.pallas_call(
        kernel,
        out_shape=(out, out),
        in_specs=[
            pl.BlockSpec(memory_space=pltpu.SMEM),
            pl.BlockSpec(memory_space=pltpu.VMEM),
            hbm, hbm, hbm, hbm,
        ],
        out_specs=(hbm, hbm),
        scratch_shapes=[
            vmem((4, LEAF, LEAF), BF16),
            vmem((WIDTH, BLOCK), BF16),
            vmem((WIDTH, BLOCK), BF16),
            vmem((2, DIM, LEAF), BF16),
            vmem((2, DIM, LEAF), BF16),
            vmem((2, DIM, LEAF), BF16),
            vmem((ROWS, BLOCK), BF16),
            vmem((2, 2, ROWS, LEAF), BF16),
            vmem((2, 2, ROWS, LEAF), BF16),
            vmem((2, 2, ROWS, LEAF), BF16),
            vmem((LEAF, DEPTH), BF16),
            vmem((2, DEPTH, LEAF), BF16),
            vmem((2, ROWS, LEAF), F32),
            vmem((2, ROWS, LEAF), F32),
            vmem((2, 8, 128), F32),
            vmem((2, 8, 128), F32),
            vmem((2, 2, HALF, WIDTH), F32),
            vmem((2, 2, HALF, WIDTH), F32),
            vmem((HALF, 384), F32),
            vmem((HALF, 384), F32),
            vmem((3, HALF, 384), F32),
            vmem((HALF, 384), BF16),
            vmem((3, HALF, 384), BF16),
            vmem((2, 2, HALF, 128), F32),
            vmem((2, 15, HALF, 128), F32),
            vmem((2, 2, HALF, 128), BF16),
            vmem((2, 2, HALF, 256), BF16),
            vmem((2, ROWS, WIDTH), BF16),
            pltpu.SemaphoreType.DMA((5,)),
            pltpu.SemaphoreType.DMA((4,)),
            pltpu.SemaphoreType.DMA((COPIES,)),
            pltpu.SemaphoreType.DMA((COPIES,)),
        ],
        compiler_params=pltpu.CompilerParams(
            collective_id=0, has_side_effects=True, vmem_limit_bytes=60 << 20
        ),
    )(
        near_leaf,
        morton.reshape(1, BLOCK),
        right_sides,
        points,
        far_left.reshape(WIDTH, BLOCK),
        far_right.reshape(WIDTH, BLOCK),
    )
    return pl.pallas_call(
        copy_out,
        out_shape=(out, out),
        in_specs=[hbm, hbm],
        out_specs=(hbm, hbm),
        scratch_shapes=[pltpu.VMEM((2, ROWS, BLOCK), F32), pltpu.SemaphoreType.DMA((2, 4))],
    )(*results)


def solution(mesh):
    placed = (
        P("rhs", "pts"),
        P("pts"),
        P("pts"),
        P(None, "pts"),
        P(None, None, "pts"),
        P(None, None, "pts"),
    )
    return jax.shard_map(
        body,
        mesh=mesh,
        in_specs=placed,
        out_specs=(P("rhs", "pts"), P("rhs", "pts")),
        check_vma=False,
    )
```
